128 devices in a mesh: shot: 16 (over y_hi, x, core), surf: 8 (over y_lo, z).
Axes of the slice: x: 4, y: 4 (y_hi: 2, y_lo: 2; y = y_hi * 2 + y_lo), z: 4, core: 2. Of those that a mesh axis runs over, the one named last changes fastest.
Arguments:
- shot_spec: bfloat16 [2, 16, 2048, 2048], P(None, None, 'shot', 'surf'), may hold values from -6 to 6
- recv_spec: bfloat16 [2, 16, 1536, 2048], P(None, None, 'shot', 'surf'), may hold values from -0.09375 to 0.09375
- wavelet: float32 [2, 16], replicated, may hold values from -4 to 4
Outputs:
- multiples: bfloat16 [2, 16, 2048, 1536], P(None, None, 'shot', 'surf')
The draws below stay inside these ranges and needn't reach their ends.
All inputs are finite; a program needn't handle non-finite values.
Results may differ from the reference program's by a relative error of at most 0.019.
Values may be sent and summed in bfloat16 or wider, within the bound.
No kernel may reach another device: no remote copies, remote signals or barrier semaphores. Data moves between devices by JAX's collectives and lax.ppermute only.
A program may use at most 128 MiB of HBM per device.

```python
import jax
import jax.numpy as jnp
from jax import lax

SHOTS = 2048
SURF = 2048
RECV = 1536
FREQ = 16
N_SURF = 8


def block_levels(rng, shape, cuts, least, largest):
    def one(dim, blocks):
        heights = jax.random.uniform(jax.random.fold_in(jax.random.fold_in(rng, 6), dim), (blocks,), jnp.float32, least / len(cuts), largest / len(cuts))
        return jnp.repeat(jnp.exp(heights), shape[dim] // blocks).reshape((-1,) + (1,) * (len(shape) - dim - 1))

    factor_of = one(*cuts[0])
    for cut in cuts[1:]:
        factor_of = factor_of * one(*cut)
    return factor_of


def centred(rng, shape, width, reach, split=(), kind=jnp.bfloat16):
    result = jax.random.normal(rng, shape, jnp.float32) * width
    if len(split) > 0:
        result = block_levels(rng, shape, split, -0.22, 0.18) * result
    return jnp.clip(result, min=-reach, max=reach).astype(kind)


def setup_inputs(seed: int = 0) -> dict:
    seeds = jax.random.split(jax.random.key(seed), 4)
    return {
        "shot_spec": centred(seeds[0], (2, FREQ, SHOTS, SURF), 1.0, 6.0, ((2, 16), (3, 8))),
        "recv_spec": centred(seeds[1], (2, FREQ, RECV, SURF), (2 * SURF) ** -0.5, 0.09375, ((2, 16), (3, 8))),
        "wavelet": centred(seeds[2], (2, FREQ), 1.0, 4.0, (), jnp.float32),
    }


def complex_product(left_factor, right_factor):
    real_term = jnp.einsum("qpu,qou->qpo", left_factor[0], right_factor[0]) - jnp.einsum("qpu,qou->qpo", left_factor[1], right_factor[1])
    imaginary_term = jnp.einsum("qpu,qou->qpo", left_factor[0], right_factor[1]) + jnp.einsum("qpu,qou->qpo", left_factor[1], right_factor[0])
    return jnp.stack([real_term, imaginary_term])


def reference(shot_spec, recv_spec, wavelet):
    group = SURF // N_SURF
    shots_f = shot_spec.astype(jnp.float32)
    recv_f = recv_spec.astype(jnp.float32)

    def add_group(total, index):
        start = (index * group).astype(jnp.int32)
        left_factor = lax.dynamic_slice_in_dim(shots_f, start, group, 3)
        right_factor = lax.dynamic_slice_in_dim(recv_f, start, group, 3)
        partial_value = complex_product(left_factor, right_factor).astype(jnp.bfloat16)
        partial_value = lax.optimization_barrier(partial_value)
        return total + partial_value.astype(jnp.float32), None

    start_total = jnp.zeros((2, FREQ, SHOTS, RECV), jnp.float32)
    summed, unused = lax.scan(add_group, start_total, jnp.arange(N_SURF, dtype=jnp.int32))
    w_real = wavelet[0][:, None, None]
    w_imag = wavelet[1][:, None, None]
    output_real = w_real * summed[0] - w_imag * summed[1]
    out_imag = w_real * summed[1] + w_imag * summed[0]
    return jnp.stack([output_real, out_imag]).astype(jnp.bfloat16)
```

```python
import functools

import jax
import jax.numpy as jnp
from jax import lax
from jax.experimental import pallas as pl
from jax.experimental.pallas import tpu as pltpu
from jax.sharding import Mesh
from jax.sharding import PartitionSpec as P

FREQUENCY = ("yh", "yl", "z")
PLACES = ("yh", "yl", "z", "c")


def product_kernel(place, wave, q_own, q_left, q_right, q_far, p_own, p_other, out):
    rows = q_own.shape[2]
    groups = q_own.shape[0] // 2
    me, frequency = place[0], place[2]
    w_real, w_imag = wave[0, frequency], wave[1, frequency]

    def apply(p_ref):
        right_factor = jnp.concatenate(
            [p_ref[j].reshape(-1, p_ref.shape[-1]) for j in range(groups)], axis=1
        )
        left_factor = jnp.concatenate(
            [
                jnp.concatenate(
                    [q[half * groups + j].reshape(2 * rows, -1) for j in range(groups)], axis=1
                )
                for q in (q_own, q_left, q_right, q_far)
                for half in range(2)
            ],
            axis=0,
        )
        terms = lax.dot_general(
            left_factor,
            right_factor,
            (((1,), (1,)), ((), ())),
            preferred_element_type=jnp.float32,
        )
        shots = terms.shape[1] // 2
        for k, step in enumerate((0, 3, 1, 2)):
            to = lax.rem(me + step, 4)
            for half in range(2):
                at = (2 * k + half) * 2 * rows
                real, imag = terms[at : at + rows], terms[at + rows : at + 2 * rows]
                s_real = real[:, :shots] - imag[:, shots:]
                s_imag = real[:, shots:] + imag[:, :shots]
                out[0, half, to, 0, 0] = (w_real * s_real - w_imag * s_imag).astype(out.dtype)
                out[0, half, to, 0, 1] = (w_real * s_imag + w_imag * s_real).astype(out.dtype)

    @pl.when(pl.program_id(0) == 0)
    def _():
        apply(p_own)

    @pl.when(pl.program_id(0) == 1)
    def _():
        apply(p_other)


def product(place, wavelet, blocks, p_own, p_other):
    sources, _, rows, depth = blocks[0].shape
    shots = p_own.shape[2]
    q_spec = pl.BlockSpec((sources, 2, rows, depth), lambda d, s, place: (0, 0, 0, 0))
    p_block = (sources // 2, 2, shots, depth)
    flops = 2 * (8 * sources // 2 * rows) * (4 * 2 * shots) * (sources // 2 * depth)
    return pl.pallas_call(
        product_kernel,
        out_shape=jax.ShapeDtypeStruct((2, 2, 4, 2, 2, rows, shots), jnp.bfloat16),
        grid_spec=pltpu.PrefetchScalarGridSpec(
            num_scalar_prefetch=1,
            grid=(2, 2),
            in_specs=[pl.BlockSpec(memory_space=pltpu.SMEM)]
            + [q_spec] * 4
            + [
                pl.BlockSpec(p_block, lambda d, s, place: (jnp.where(d == 0, s, 1), 0, 0, 0)),
                pl.BlockSpec(p_block, lambda d, s, place: (jnp.where(d == 1, s, 0), 0, 0, 0)),
            ],
            out_specs=pl.BlockSpec(
                (1, 2, 4, 1, 2, rows, shots),
                lambda d, s, place: (s, 0, 0, lax.rem(place[1] + d, 2), 0, 0, 0),
            ),
        ),
        compiler_params=pltpu.CompilerParams(vmem_limit_bytes=48 * 2**20),
        cost_estimate=pl.CostEstimate(
            flops=flops,
            bytes_accessed=2 * (4 * blocks[0].size + 2 * p_own.size + 32 * 2 * rows * shots),
            transcendentals=0,
        ),
    )(place, wavelet, *blocks, p_own, p_other)


def shift(value, axis, size, step):
    return lax.ppermute(value, axis, [(i, (i + step) % size) for i in range(size)])


def by_frequency(value):
    return lax.all_to_all(value, FREQUENCY, 0, 0, tiled=True)


def on_device(shot_spec, recv_spec, wavelet):
    place = jnp.stack(
        [lax.axis_index("x"), lax.axis_index("c"), lax.axis_index(FREQUENCY)]
    ).astype(jnp.int32)
    half = recv_spec.shape[2] // 2
    recv = by_frequency(recv_spec.swapaxes(0, 1))
    first, second = recv[:, :, :half], recv[:, :, half:]
    first_left, first_right = shift(first, "x", 4, 1), shift(first, "x", 4, -1)
    first_far = shift(first_left, "x", 4, 1)
    second_left, second_right = shift(second, "x", 4, 1), shift(second, "x", 4, -1)
    second_far = shift(second_right, "x", 4, -1)
    shots = by_frequency(shot_spec.swapaxes(0, 1))
    other = shift(shots, "c", 2, 1)
    parts = []
    for blocks in (
        (first, first_left, first_right, first_far),
        (second, second_left, second_right, second_far),
    ):
        out = product(place, wavelet, blocks, shots, other)
        out = out.reshape((-1,) + out.shape[4:])
        out = lax.all_to_all(out, PLACES, 0, 0, tiled=True)
        out = out.reshape((out.shape[0] // 2, 2) + out.shape[1:])
        parts.append(out.transpose(2, 0, 1, 3, 4))
    out = jnp.concatenate(parts, axis=3)
    out = out.reshape(out.shape[:2] + (-1, out.shape[-1]))
    return out.swapaxes(2, 3)


def solution(mesh):
    devices = mesh.devices.reshape(2, 4, 2, 2, 4)
    wide = Mesh(devices, ("yh", "x", "c", "yl", "z"))
    spec = P(None, None, ("yh", "x", "c"), ("yl", "z"))
    return jax.shard_map(
        on_device, mesh=wide, in_specs=(spec, spec, P()), out_specs=spec, check_vma=False
    )
```

```python
import functools

import jax
import jax.numpy as jnp
from jax import lax
from jax.experimental import pallas as pl
from jax.experimental.pallas import tpu as pltpu
from jax.sharding import Mesh
from jax.sharding import PartitionSpec as P

FREQUENCY = ("yh", "yl", "z")
PLACES = ("yh", "yl", "z", "c")
ORDER = 10**11


def product_kernel(steps, place, wave, *refs):
    count = 2 * len(steps)
    pieces, (p_own, p_other), out = refs[:count], refs[count : count + 2], refs[-1]
    groups = p_own.shape[0] // 2
    shots = p_own.shape[2]
    x, core, frequency = place[0], place[1], place[2]
    w_real, w_imag = wave[0, frequency], wave[1, frequency]

    def rows_of(piece, half):
        return jnp.concatenate(
            [
                piece[half * groups + j].reshape(-1, piece.shape[3])
                for j in range(groups)
            ],
            axis=1,
        )

    for distance, p_ref in enumerate((p_own, p_other)):
        to_core = lax.rem(core + distance, 2)
        for p_half in range(2):
            right_factor = rows_of(p_ref, p_half)
            left_factor = jnp.concatenate(
                [rows_of(piece, half) for piece in pieces for half in range(2)], axis=0
            )
            terms = lax.dot_general(
                left_factor,
                right_factor,
                (((1,), (1,)), ((), ())),
                preferred_element_type=jnp.float32,
            )
            at = 0
            for k, piece in enumerate(pieces):
                rows = piece.shape[2]
                to = lax.rem(x + steps[k // 2], 4)
                low = 0 if k % 2 == 0 else pieces[k - 1].shape[2]
                for half in range(2):
                    real, imag = terms[at : at + rows], terms[at + rows : at + 2 * rows]
                    at += 2 * rows
                    s_real = real[:, :shots] - imag[:, shots:]
                    s_imag = real[:, shots:] + imag[:, :shots]
                    out[p_half, half, to, to_core, 0, low : low + rows] = (
                        w_real * s_real - w_imag * s_imag
                    ).astype(out.dtype)
                    out[p_half, half, to, to_core, 1, low : low + rows] = (
                        w_real * s_imag + w_imag * s_real
                    ).astype(out.dtype)


def product(place, wavelet, steps, pieces, p_own, p_other, earlier=None):
    sources, _, _, depth = pieces[0].shape
    rows = pieces[0].shape[2] + pieces[1].shape[2]
    shots = p_own.shape[2]
    vmem = pl.BlockSpec(memory_space=pltpu.VMEM)
    smem = pl.BlockSpec(memory_space=pltpu.SMEM)
    operands = [place, wavelet, *pieces, p_own, p_other]
    specs = [smem, smem] + [vmem] * (len(pieces) + 2)
    kernel = functools.partial(product_kernel, steps)
    aliases = {}
    if earlier is not None:
        aliases = {len(operands): 0}
        operands.append(earlier)
        specs.append(vmem)
    flops = 2 * (2 * rows * len(steps) * 2) * (4 * 2 * shots) * (sources // 2 * depth)
    return pl.pallas_call(
        kernel,
        out_shape=jax.ShapeDtypeStruct((2, 2, 4, 2, 2, rows, shots), jnp.bfloat16),
        in_specs=specs,
        out_specs=vmem,
        input_output_aliases=aliases,
        compiler_params=pltpu.CompilerParams(vmem_limit_bytes=32 * 2**20),
        cost_estimate=pl.CostEstimate(flops=flops, bytes_accessed=2**20, transcendentals=0),
    )(*operands)


def ordered_kernel(source, out):
    pass


def ordered(value):
    return pl.pallas_call(
        ordered_kernel,
        out_shape=jax.ShapeDtypeStruct(value.shape, value.dtype),
        in_specs=[pl.BlockSpec(memory_space=pl.ANY)],
        out_specs=pl.BlockSpec(memory_space=pl.ANY),
        input_output_aliases={0: 0},
        cost_estimate=pl.CostEstimate(flops=ORDER, bytes_accessed=0, transcendentals=0),
    )(value)


def shift(value, axis, size, step):
    return lax.ppermute(value, axis, [(i, (i + step) % size) for i in range(size)])


def by_frequency(value):
    return lax.all_to_all(value, FREQUENCY, 0, 0, tiled=True)


def on_device(shot_spec, recv_spec, wavelet):
    place = jnp.stack(
        [lax.axis_index("x"), lax.axis_index("c"), lax.axis_index(FREQUENCY)]
    ).astype(jnp.int32)
    half = recv_spec.shape[2] // 2
    recv = by_frequency(recv_spec.swapaxes(0, 1))
    recv, shot_spec = lax.optimization_barrier((recv, shot_spec))
    first, second = recv[:, :, :half], recv[:, :, half:]
    first_left, first_right = shift(first, "x", 4, 1), shift(first, "x", 4, -1)
    first_left = ordered(first_left)
    first_far = shift(first_left, "x", 4, 1)
    second_left, second_right = shift(second, "x", 4, 1), shift(second, "x", 4, -1)
    second_right = ordered(second_right)
    second_far = shift(second_right, "x", 4, -1)
    shots = by_frequency(shot_spec.swapaxes(0, 1))
    other = shift(shots, "c", 2, 1)
    near = (first, second, first_left, second_left, first_right, second_right)
    out = product(place, wavelet, (0, 3, 1), near, shots, other)
    out = product(place, wavelet, (2,), (first_far, second_far), shots, other, out)
    out = out.reshape((-1,) + out.shape[4:])
    out = lax.all_to_all(out, PLACES, 0, 0, tiled=True)
    out = out.reshape((out.shape[0] // 2, 2) + out.shape[1:])
    out = out.transpose(2, 0, 1, 3, 4)
    out = out.reshape(out.shape[:2] + (-1, out.shape[-1]))
    return out.swapaxes(2, 3)


def solution(mesh):
    devices = mesh.devices.reshape(2, 4, 2, 2, 4)
    wide = Mesh(devices, ("yh", "x", "c", "yl", "z"))
    spec = P(None, None, ("yh", "x", "c"), ("yl", "z"))
    return jax.shard_map(
        on_device, mesh=wide, in_specs=(spec, spec, P()), out_specs=spec, check_vma=False
    )
```

```python
import functools

import jax
import jax.numpy as jnp
from jax import lax
from jax.experimental import pallas as pl
from jax.experimental.pallas import tpu as pltpu
from jax.sharding import Mesh
from jax.sharding import PartitionSpec as P

FREQUENCY = ("yh", "yl", "z")
PLACES = ("yh", "yl", "z", "c")
ORDER = 10**11


def product_kernel(steps, place, wave, *refs):
    count = 2 * len(steps)
    pieces, (p_own, p_other), out = refs[:count], refs[count : count + 2], refs[-1]
    groups = p_own.shape[0] // 2
    shots = p_own.shape[2]
    x, core, frequency = place[0], place[1], place[2]
    w_real, w_imag = wave[0, frequency], wave[1, frequency]

    def rows_of(piece, half):
        return jnp.concatenate(
            [
                piece[half * groups + j].reshape(-1, piece.shape[3])
                for j in range(groups)
            ],
            axis=1,
        )

    for distance, p_ref in enumerate((p_own, p_other)):
        to_core = lax.rem(core + distance, 2)
        for p_half in range(2):
            right_factor = rows_of(p_ref, p_half)
            left_factor = jnp.concatenate(
                [rows_of(piece, half) for piece in pieces for half in range(2)], axis=0
            )
            terms = lax.dot_general(
                left_factor,
                right_factor,
                (((1,), (1,)), ((), ())),
                preferred_element_type=jnp.float32,
            )
            at = 0
            for k, piece in enumerate(pieces):
                rows = piece.shape[2]
                to = lax.rem(x + steps[k // 2], 4)
                low = 0 if k % 2 == 0 else pieces[k - 1].shape[2]
                for half in range(2):
                    real, imag = terms[at : at + rows], terms[at + rows : at + 2 * rows]
                    at += 2 * rows
                    s_real = real[:, :shots] - imag[:, shots:]
                    s_imag = real[:, shots:] + imag[:, :shots]
                    out[p_half, half, to, to_core, 0, low : low + rows] = (
                        w_real * s_real - w_imag * s_imag
                    ).astype(out.dtype)
                    out[p_half, half, to, to_core, 1, low : low + rows] = (
                        w_real * s_imag + w_imag * s_real
                    ).astype(out.dtype)


def product(place, wavelet, blocks, p_own, p_other, earlier=None):
    steps = tuple(blocks)
    pieces = [piece for pair in blocks.values() for piece in pair]
    sources, _, _, depth = pieces[0].shape
    rows = pieces[0].shape[2] + pieces[1].shape[2]
    shots = p_own.shape[2]
    vmem = pl.BlockSpec(memory_space=pltpu.VMEM)
    smem = pl.BlockSpec(memory_space=pltpu.SMEM)
    operands = [place, wavelet, *pieces, p_own, p_other]
    specs = [smem, smem] + [vmem] * (len(pieces) + 2)
    kernel = functools.partial(product_kernel, steps)
    aliases = {}
    if earlier is not None:
        aliases = {len(operands): 0}
        operands.append(earlier)
        specs.append(vmem)
    flops = 2 * (2 * rows * len(steps) * 2) * (4 * 2 * shots) * (sources // 2 * depth)
    return pl.pallas_call(
        kernel,
        out_shape=jax.ShapeDtypeStruct((2, 2, 4, 2, 2, rows, shots), jnp.bfloat16),
        in_specs=specs,
        out_specs=vmem,
        input_output_aliases=aliases,
        compiler_params=pltpu.CompilerParams(vmem_limit_bytes=32 * 2**20),
        cost_estimate=pl.CostEstimate(flops=flops, bytes_accessed=2**20, transcendentals=0),
    )(*operands)


def ordered_kernel(source, out):
    pass


def ordered(value):
    return pl.pallas_call(
        ordered_kernel,
        out_shape=jax.ShapeDtypeStruct(value.shape, value.dtype),
        in_specs=[pl.BlockSpec(memory_space=pl.ANY)],
        out_specs=pl.BlockSpec(memory_space=pl.ANY),
        input_output_aliases={0: 0},
        cost_estimate=pl.CostEstimate(flops=ORDER, bytes_accessed=0, transcendentals=0),
    )(value)


def shift(value, axis, size, step):
    return lax.ppermute(value, axis, [(i, (i + step) % size) for i in range(size)])


def by_frequency(value):
    return lax.all_to_all(value, FREQUENCY, 0, 0, tiled=True)


def on_device(shot_spec, recv_spec, wavelet):
    place = jnp.stack(
        [lax.axis_index("x"), lax.axis_index("c"), lax.axis_index(FREQUENCY)]
    ).astype(jnp.int32)
    half = recv_spec.shape[2] // 2
    recv = by_frequency(recv_spec.swapaxes(0, 1))
    recv, shot_spec = lax.optimization_barrier((recv, shot_spec))
    first, second = recv[:, :, :half], recv[:, :, half:]
    first_left, second_right = shift(first, "x", 4, 1), shift(second, "x", 4, -1)
    first_left, second_right = ordered(first_left), ordered(second_right)
    first_far, second_far = shift(first_left, "x", 4, 1), shift(second_right, "x", 4, -1)
    first_right, second_left = ordered(shift(first, "x", 4, -1)), ordered(shift(second, "x", 4, 1))
    shots = by_frequency(shot_spec.swapaxes(0, 1))
    other = shift(shots, "c", 2, 1)
    near = {0: (first, second), 3: (first_left, second_left), 1: (first_right, second_right)}
    far = {2: (first_far, second_far)}
    out = product(place, wavelet, near, shots, other)
    out = product(place, wavelet, far, shots, other, out)
    out = out.reshape((-1,) + out.shape[4:])
    out = lax.all_to_all(out, PLACES, 0, 0, tiled=True)
    out = out.reshape((out.shape[0] // 2, 2) + out.shape[1:])
    out = out.transpose(2, 0, 1, 3, 4)
    out = out.reshape(out.shape[:2] + (-1, out.shape[-1]))
    return out.swapaxes(2, 3)


def solution(mesh):
    devices = mesh.devices.reshape(2, 4, 2, 2, 4)
    wide = Mesh(devices, ("yh", "x", "c", "yl", "z"))
    spec = P(None, None, ("yh", "x", "c"), ("yl", "z"))
    return jax.shard_map(
        on_device, mesh=wide, in_specs=(spec, spec, P()), out_specs=spec, check_vma=False
    )
```

```python
import functools

import jax
import jax.numpy as jnp
from jax import lax
from jax.experimental import pallas as pl
from jax.experimental.pallas import tpu as pltpu
from jax.sharding import Mesh
from jax.sharding import PartitionSpec as P

FREQUENCY = ("yh", "yl", "z")
PLACES = ("yh", "yl", "z", "c")
ORDER = 10**11


def rows_of(piece, half):
    groups = piece.shape[0] // 2
    return jnp.concatenate(
        [piece[half * groups + j].reshape(-1, piece.shape[3]) for j in range(groups)], axis=1
    )


def emit(terms, steps, pieces, p_half, to_core, place, wave, out):
    shots = terms.shape[1] // 2
    x, frequency = place[0], place[2]
    w_real, w_imag = wave[0, frequency], wave[1, frequency]
    at = 0
    for k, piece in enumerate(pieces):
        rows = piece.shape[2]
        to = lax.rem(x + steps[k // 2], 4)
        low = 0 if k % 2 == 0 else pieces[k - 1].shape[2]
        for half in range(2):
            real, imag = terms[at : at + rows], terms[at + rows : at + 2 * rows]
            at += 2 * rows
            s_real = real[:, :shots] - imag[:, shots:]
            s_imag = real[:, shots:] + imag[:, :shots]
            out[p_half, half, to, to_core, 0, low : low + rows] = (
                w_real * s_real - w_imag * s_imag
            ).astype(out.dtype)
            out[p_half, half, to, to_core, 1, low : low + rows] = (
                w_real * s_imag + w_imag * s_real
            ).astype(out.dtype)


def product_kernel(steps, place, wave, *refs):
    pieces, factors = refs[: 2 * len(steps)], refs[2 * len(steps) :]
    out = factors[-1] if len(factors) == 3 else factors[-2]
    for distance in range(2):
        to_core = lax.rem(place[1] + distance, 2)
        for p_half in range(2):
            if len(factors) == 4:
                right_factor = rows_of(factors[distance], p_half)
                factors[-1][distance, p_half] = right_factor
            else:
                right_factor = factors[0][distance, p_half]
            left_factor = jnp.concatenate(
                [rows_of(piece, half) for piece in pieces for half in range(2)], axis=0
            )
            terms = lax.dot_general(
                left_factor,
                right_factor,
                (((1,), (1,)), ((), ())),
                preferred_element_type=jnp.float32,
            )
            emit(terms, steps, pieces, p_half, to_core, place, wave, out)


def product(place, wavelet, blocks, factors, earlier=None):
    steps = tuple(blocks)
    pieces = [piece for pair in blocks.values() for piece in pair]
    depth = pieces[0].shape[0] // 2 * pieces[0].shape[3]
    rows = pieces[0].shape[2] + pieces[1].shape[2]
    shots = factors[0].shape[2] if earlier is None else factors[0].shape[2] // 2
    vmem = pl.BlockSpec(memory_space=pltpu.VMEM)
    smem = pl.BlockSpec(memory_space=pltpu.SMEM)
    operands = [place, wavelet, *pieces, *factors]
    shape = jax.ShapeDtypeStruct((2, 2, 4, 2, 2, rows, shots), jnp.bfloat16)
    aliases = {}
    if earlier is None:
        shape = (shape, jax.ShapeDtypeStruct((2, 2, 2 * shots, depth), jnp.bfloat16))
    else:
        aliases = {len(operands): 0}
        operands.append(earlier)
    flops = 2 * (4 * rows * len(steps)) * (8 * shots) * depth
    return pl.pallas_call(
        functools.partial(product_kernel, steps),
        out_shape=shape,
        in_specs=[smem, smem] + [vmem] * (len(operands) - 2),
        out_specs=(vmem, vmem) if earlier is None else vmem,
        input_output_aliases=aliases,
        compiler_params=pltpu.CompilerParams(vmem_limit_bytes=32 * 2**20),
        cost_estimate=pl.CostEstimate(flops=flops, bytes_accessed=2**20, transcendentals=0),
    )(*operands)


def moves_kernel(pairs, source, *refs):
    outs, done = refs[:-1], refs[-1]
    copies = [
        pltpu.make_async_copy(source.at[a], outs[k].at[b], done.at[i])
        for i, (a, k, b) in enumerate(pairs)
    ]
    for copy in copies:
        copy.start()
    for copy in copies:
        copy.wait()


def moves(value, pairs, shapes, source_space, out_space):
    outs = [jax.ShapeDtypeStruct(shape, value.dtype) for shape in shapes]
    return pl.pallas_call(
        functools.partial(moves_kernel, pairs),
        out_shape=outs,
        in_specs=[pl.BlockSpec(memory_space=source_space)],
        out_specs=[pl.BlockSpec(memory_space=out_space)] * len(outs),
        scratch_shapes=[pltpu.SemaphoreType.DMA((len(pairs),))],
        compiler_params=pltpu.CompilerParams(vmem_limit_bytes=8 * 2**20),
        cost_estimate=pl.CostEstimate(
            flops=0, bytes_accessed=2 * value.size * value.dtype.itemsize, transcendentals=0
        ),
    )(value)


def ordered_kernel(source, out):
    pass


def ordered(value):
    return pl.pallas_call(
        ordered_kernel,
        out_shape=jax.ShapeDtypeStruct(value.shape, value.dtype),
        in_specs=[pl.BlockSpec(memory_space=pl.ANY)],
        out_specs=pl.BlockSpec(memory_space=pl.ANY),
        input_output_aliases={0: 0},
        cost_estimate=pl.CostEstimate(flops=ORDER, bytes_accessed=0, transcendentals=0),
    )(value)


def shift(value, axis, size, step):
    return lax.ppermute(value, axis, [(i, (i + step) % size) for i in range(size)])


def by_frequency(value):
    return lax.all_to_all(value, FREQUENCY, 0, 0, tiled=True)


def on_device(shot_spec, recv_spec, wavelet):
    place = jnp.stack(
        [lax.axis_index("x"), lax.axis_index("c"), lax.axis_index(FREQUENCY)]
    ).astype(jnp.int32)
    rows, depth = recv_spec.shape[2:]
    half = rows // 2
    every = slice(None)
    (recv,) = moves(
        recv_spec,
        [(part, 0, (every, part)) for part in range(2)],
        [(16, 2, rows, depth)],
        pltpu.HBM,
        pltpu.VMEM,
    )
    recv = by_frequency(recv)
    recv, shot_spec = lax.optimization_barrier((recv, shot_spec))
    first, second = moves(
        recv,
        [((every, every, pl.ds(k * half, half)), k, every) for k in range(2)],
        [(16, 2, half, depth)] * 2,
        pltpu.VMEM,
        pl.ANY,
    )
    first_left, second_right = shift(first, "x", 4, 1), shift(second, "x", 4, -1)
    first_left, second_right = ordered(first_left), ordered(second_right)
    first_far, second_far = shift(first_left, "x", 4, 1), shift(second_right, "x", 4, -1)
    first_right, second_left = ordered(shift(first, "x", 4, -1)), ordered(shift(second, "x", 4, 1))
    shots = by_frequency(shot_spec.swapaxes(0, 1))
    other = shift(shots, "c", 2, 1)
    near = {0: (first, second), 3: (first_left, second_left), 1: (first_right, second_right)}
    far = {2: (first_far, second_far)}
    out, packed = product(place, wavelet, near, (shots, other))
    out = product(place, wavelet, far, (packed,), out)
    out = out.reshape((-1,) + out.shape[4:])
    out = lax.all_to_all(out, PLACES, 0, 0, tiled=True)
    out = out.reshape((out.shape[0] // 2, 2) + out.shape[1:])
    (out,) = moves(
        out,
        [((every, every, part), 0, part) for part in range(2)],
        [(2,) + out.shape[:2] + out.shape[3:]],
        pltpu.VMEM,
        pl.ANY,
    )
    out = out.reshape(out.shape[:2] + (-1, out.shape[-1]))
    return out.swapaxes(2, 3)


def solution(mesh):
    devices = mesh.devices.reshape(2, 4, 2, 2, 4)
    wide = Mesh(devices, ("yh", "x", "c", "yl", "z"))
    spec = P(None, None, ("yh", "x", "c"), ("yl", "z"))
    return jax.shard_map(
        on_device, mesh=wide, in_specs=(spec, spec, P()), out_specs=spec, check_vma=False
    )
```

```python
import functools

import jax
import jax.numpy as jnp
from jax import lax
from jax.experimental import pallas as pl
from jax.experimental.pallas import tpu as pltpu
from jax.sharding import Mesh
from jax.sharding import PartitionSpec as P

FREQUENCY = ("yh", "yl", "z")
PLACES = ("yh", "yl", "z", "c")
ORDER = 2 * 10**10


def rows_of(piece, half):
    groups = piece.shape[0] // 2
    return jnp.concatenate(
        [piece[half * groups + j].reshape(-1, piece.shape[3]) for j in range(groups)], axis=1
    )


def emit(terms, spots, pieces, p_half, to_core, place, wave, out):
    shots = terms.shape[1] // 2
    x, frequency = place[0], place[2]
    w_real, w_imag = wave[0, frequency], wave[1, frequency]
    at = 0
    for (step, low), piece in zip(spots, pieces):
        rows = piece.shape[2]
        to = lax.rem(x + step, 4)
        for half in range(2):
            real, imag = terms[at : at + rows], terms[at + rows : at + 2 * rows]
            at += 2 * rows
            s_real = real[:, :shots] - imag[:, shots:]
            s_imag = real[:, shots:] + imag[:, :shots]
            out[p_half, half, to, to_core, 0, low : low + rows] = (
                w_real * s_real - w_imag * s_imag
            ).astype(out.dtype)
            out[p_half, half, to, to_core, 1, low : low + rows] = (
                w_real * s_imag + w_imag * s_real
            ).astype(out.dtype)


def product_kernel(spots, distances, pack, earlier, place, wave, *refs):
    pieces, refs = refs[: len(spots)], refs[len(spots) :]
    factors = refs[: len(distances)]
    out, *packed = refs[len(distances) + earlier :]
    for distance, factor in zip(distances, factors):
        to_core = lax.rem(place[1] + distance, 2)
        for p_half in range(2):
            if len(factor.shape) == 4:
                right_factor = rows_of(factor, p_half)
            else:
                right_factor = factor[p_half]
            if pack:
                packed[distance - distances[0]][p_half] = right_factor
            left_factor = jnp.concatenate(
                [rows_of(piece, half) for piece in pieces for half in range(2)], axis=0
            )
            terms = lax.dot_general(
                left_factor,
                right_factor,
                (((1,), (1,)), ((), ())),
                preferred_element_type=jnp.float32,
            )
            emit(terms, spots, pieces, p_half, to_core, place, wave, out)


def product(place, wavelet, blocks, factors, rows, earlier=None, pack=False):
    spots, pieces = tuple(blocks), list(blocks.values())
    distances, factors = tuple(factors), list(factors.values())
    depth = pieces[0].shape[0] // 2 * pieces[0].shape[3]
    shots = factors[0].shape[2] if factors[0].ndim == 4 else factors[0].shape[1] // 2
    vmem = pl.BlockSpec(memory_space=pltpu.VMEM)
    smem = pl.BlockSpec(memory_space=pltpu.SMEM)
    operands = [place, wavelet, *pieces, *factors]
    shapes = [jax.ShapeDtypeStruct((2, 2, 4, 2, 2, rows, shots), jnp.bfloat16)]
    if pack:
        shapes += [jax.ShapeDtypeStruct((2, 2 * shots, depth), jnp.bfloat16)] * len(factors)
    aliases = {}
    if earlier is not None:
        aliases = {len(operands): 0}
        operands.append(earlier)
    count = sum(piece.shape[2] for piece in pieces)
    flops = 2 * (4 * count) * (4 * shots * len(factors)) * depth
    return pl.pallas_call(
        functools.partial(product_kernel, spots, distances, pack, len(aliases)),
        out_shape=shapes,
        in_specs=[smem, smem] + [vmem] * (len(operands) - 2),
        out_specs=[vmem] * len(shapes),
        input_output_aliases=aliases,
        compiler_params=pltpu.CompilerParams(vmem_limit_bytes=28 * 2**20),
        cost_estimate=pl.CostEstimate(flops=flops, bytes_accessed=2**20, transcendentals=0),
    )(*operands)


def moves_kernel(pairs, count, *refs):
    sources, outs, done = refs[:count], refs[count:-1], refs[-1]
    copies = [
        pltpu.make_async_copy(sources[n].at[a], outs[k].at[b], done.at[i])
        for i, (n, a, k, b) in enumerate(pairs)
    ]
    for copy in copies:
        copy.start()
    for copy in copies:
        copy.wait()


def moves(values, pairs, shapes, source_space, out_space):
    outs = [jax.ShapeDtypeStruct(shape, values[0].dtype) for shape in shapes]
    return pl.pallas_call(
        functools.partial(moves_kernel, pairs, len(values)),
        out_shape=outs,
        in_specs=[pl.BlockSpec(memory_space=source_space)] * len(values),
        out_specs=[pl.BlockSpec(memory_space=out_space)] * len(outs),
        scratch_shapes=[pltpu.SemaphoreType.DMA((len(pairs),))],
        compiler_params=pltpu.CompilerParams(vmem_limit_bytes=8 * 2**20),
        cost_estimate=pl.CostEstimate(
            flops=0, bytes_accessed=4 * sum(value.size for value in values), transcendentals=0
        ),
    )(*values)


def ordered_kernel(source, out):
    pass


def ordered(value):
    return pl.pallas_call(
        ordered_kernel,
        out_shape=jax.ShapeDtypeStruct(value.shape, value.dtype),
        in_specs=[pl.BlockSpec(memory_space=pl.ANY)],
        out_specs=pl.BlockSpec(memory_space=pl.ANY),
        input_output_aliases={0: 0},
        cost_estimate=pl.CostEstimate(flops=ORDER, bytes_accessed=0, transcendentals=0),
    )(value)


def shift(value, axis, size, step):
    return lax.ppermute(value, axis, [(i, (i + step) % size) for i in range(size)])


def by_frequency(value):
    return lax.all_to_all(value, FREQUENCY, 0, 0, tiled=True)


def on_device(shot_spec, recv_spec, wavelet):
    place = jnp.stack(
        [lax.axis_index("x"), lax.axis_index("c"), lax.axis_index(FREQUENCY)]
    ).astype(jnp.int32)
    rows, depth = recv_spec.shape[2:]
    every = slice(None)
    (recv,) = moves(
        [recv_spec],
        [(0, part, 0, (every, part)) for part in range(2)],
        [(16, 2, rows, depth)],
        pltpu.HBM,
        pltpu.VMEM,
    )
    recv = by_frequency(recv)
    recv, shot_spec = lax.optimization_barrier((recv, shot_spec))
    half = rows // 2
    first, second = moves(
        [recv],
        [(0, (every, every, pl.ds(k * half, half)), k, every) for k in range(2)],
        [(16, 2, half, depth)] * 2,
        pltpu.VMEM,
        pl.ANY,
    )
    first_left, second_right = shift(first, "x", 4, 1), shift(second, "x", 4, -1)
    first_left, second_right = ordered(first_left), ordered(second_right)
    far = {(2, 0): shift(first_left, "x", 4, 1), (2, half): shift(second_right, "x", 4, -1)}
    first_right = ordered(shift(first, "x", 4, -1))
    second_left = ordered(shift(second, "x", 4, 1))
    shots = by_frequency(shot_spec.swapaxes(0, 1))
    other = shift(shots, "c", 2, 1)
    near = {(0, 0): first, (0, half): second, (3, 0): first_left, (3, half): second_left}
    near |= {(1, 0): first_right, (1, half): second_right}
    out, own_p = product(place, wavelet, near, {0: shots}, rows, pack=True)
    out, other_p = product(place, wavelet, near, {1: other}, rows, out, pack=True)
    factors = {0: own_p, 1: other_p}
    (out,) = product(place, wavelet, far, factors, rows, out)
    out = back(out)
    (out,) = moves(
        [out],
        [(0, (every, every, part), 0, part) for part in range(2)],
        [(2,) + out.shape[:2] + out.shape[3:]],
        pltpu.VMEM,
        pl.ANY,
    )
    out = out.reshape(out.shape[:2] + (-1, out.shape[-1]))
    return out.swapaxes(2, 3)


def back(out):
    out = out.reshape((-1,) + out.shape[4:])
    out = lax.all_to_all(out, PLACES, 0, 0, tiled=True)
    return out.reshape((out.shape[0] // 2, 2) + out.shape[1:])


def solution(mesh):
    devices = mesh.devices.reshape(2, 4, 2, 2, 4)
    wide = Mesh(devices, ("yh", "x", "c", "yl", "z"))
    spec = P(None, None, ("yh", "x", "c"), ("yl", "z"))
    return jax.shard_map(
        on_device, mesh=wide, in_specs=(spec, spec, P()), out_specs=spec, check_vma=False
    )
```

```python
import functools

import jax
import jax.numpy as jnp
from jax import lax
from jax.experimental import pallas as pl
from jax.experimental.pallas import tpu as pltpu
from jax.sharding import Mesh
from jax.sharding import PartitionSpec as P

FREQUENCY = ("yh", "yl", "z")
PLACES = ("yh", "yl", "c", "z")
ORDER = 2 * 10**10


def rows_of(piece, half):
    groups = piece.shape[0] // 2
    return jnp.concatenate(
        [piece[half * groups + j].reshape(-1, piece.shape[3]) for j in range(groups)], axis=1
    )


def emit(terms, spots, pieces, p_half, to_core, place, wave, out):
    shots = terms.shape[1] // 2
    x, frequency = place[0], place[2]
    w_real, w_imag = wave[0, frequency], wave[1, frequency]
    at = 0
    for (step, low), piece in zip(spots, pieces):
        rows = piece.shape[2]
        to = lax.rem(x + step, 4)
        for half in range(2):
            real, imag = terms[at : at + rows], terms[at + rows : at + 2 * rows]
            at += 2 * rows
            s_real = real[:, :shots] - imag[:, shots:]
            s_imag = real[:, shots:] + imag[:, :shots]
            out[p_half, half, to_core, to, 0, low : low + rows] = (
                w_real * s_real - w_imag * s_imag
            ).astype(out.dtype)
            out[p_half, half, to_core, to, 1, low : low + rows] = (
                w_real * s_imag + w_imag * s_real
            ).astype(out.dtype)


def product_kernel(spots, distances, pack, earlier, place, wave, *refs):
    pieces, refs = refs[: len(spots)], refs[len(spots) :]
    factors = refs[: len(distances)]
    out, *packed = refs[len(distances) + earlier :]
    for distance, factor in zip(distances, factors):
        to_core = lax.rem(place[1] + distance, 2)
        for p_half in range(2):
            if len(factor.shape) == 4:
                right_factor = rows_of(factor, p_half)
            else:
                right_factor = factor[p_half]
            if pack:
                packed[distance - distances[0]][p_half] = right_factor
            left_factor = jnp.concatenate(
                [rows_of(piece, half) for piece in pieces for half in range(2)], axis=0
            )
            terms = lax.dot_general(
                left_factor,
                right_factor,
                (((1,), (1,)), ((), ())),
                preferred_element_type=jnp.float32,
            )
            emit(terms, spots, pieces, p_half, to_core, place, wave, out)


def product(place, wavelet, blocks, factors, rows, earlier=None, pack=False):
    spots, pieces = tuple(blocks), list(blocks.values())
    distances, factors = tuple(factors), list(factors.values())
    depth = pieces[0].shape[0] // 2 * pieces[0].shape[3]
    shots = factors[0].shape[2] if factors[0].ndim == 4 else factors[0].shape[1] // 2
    vmem = pl.BlockSpec(memory_space=pltpu.VMEM)
    smem = pl.BlockSpec(memory_space=pltpu.SMEM)
    operands = [place, wavelet, *pieces, *factors]
    shapes = [jax.ShapeDtypeStruct((2, 2, 2, 4, 2, rows, shots), jnp.bfloat16)]
    if pack:
        shapes += [jax.ShapeDtypeStruct((2, 2 * shots, depth), jnp.bfloat16)] * len(factors)
    aliases = {}
    if earlier is not None:
        aliases = {len(operands): 0}
        operands.append(earlier)
    count = sum(piece.shape[2] for piece in pieces)
    flops = 2 * (4 * count) * (4 * shots * len(factors)) * depth
    return pl.pallas_call(
        functools.partial(product_kernel, spots, distances, pack, len(aliases)),
        out_shape=shapes,
        in_specs=[smem, smem] + [vmem] * (len(operands) - 2),
        out_specs=[vmem] * len(shapes),
        input_output_aliases=aliases,
        compiler_params=pltpu.CompilerParams(vmem_limit_bytes=28 * 2**20),
        cost_estimate=pl.CostEstimate(flops=flops, bytes_accessed=2**20, transcendentals=0),
    )(*operands)


def moves_kernel(pairs, count, *refs):
    sources, outs, done = refs[:count], refs[count:-1], refs[-1]
    copies = [
        pltpu.make_async_copy(sources[n].at[a], outs[k].at[b], done.at[i])
        for i, (n, a, k, b) in enumerate(pairs)
    ]
    for copy in copies:
        copy.start()
    for copy in copies:
        copy.wait()


def moves(values, pairs, shapes, source_space, out_space):
    outs = [jax.ShapeDtypeStruct(shape, values[0].dtype) for shape in shapes]
    return pl.pallas_call(
        functools.partial(moves_kernel, pairs, len(values)),
        out_shape=outs,
        in_specs=[pl.BlockSpec(memory_space=source_space)] * len(values),
        out_specs=[pl.BlockSpec(memory_space=out_space)] * len(outs),
        scratch_shapes=[pltpu.SemaphoreType.DMA((len(pairs),))],
        compiler_params=pltpu.CompilerParams(vmem_limit_bytes=8 * 2**20),
        cost_estimate=pl.CostEstimate(
            flops=0, bytes_accessed=4 * sum(value.size for value in values), transcendentals=0
        ),
    )(*values)


def ordered_kernel(source, out):
    pass


def ordered(value):
    return pl.pallas_call(
        ordered_kernel,
        out_shape=jax.ShapeDtypeStruct(value.shape, value.dtype),
        in_specs=[pl.BlockSpec(memory_space=pl.ANY)],
        out_specs=pl.BlockSpec(memory_space=pl.ANY),
        input_output_aliases={0: 0},
        cost_estimate=pl.CostEstimate(flops=ORDER, bytes_accessed=0, transcendentals=0),
    )(value)


def shift(value, axis, size, step):
    return lax.ppermute(value, axis, [(i, (i + step) % size) for i in range(size)])


def by_frequency(value):
    return lax.all_to_all(value, FREQUENCY, 0, 0, tiled=True)


def on_device(shot_spec, recv_spec, wavelet):
    place = jnp.stack(
        [lax.axis_index("x"), lax.axis_index("c"), lax.axis_index(FREQUENCY)]
    ).astype(jnp.int32)
    rows, depth = recv_spec.shape[2:]
    every = slice(None)
    (recv,) = moves(
        [recv_spec],
        [(0, part, 0, (every, part)) for part in range(2)],
        [(16, 2, rows, depth)],
        pltpu.HBM,
        pltpu.VMEM,
    )
    recv = by_frequency(recv)
    recv, shot_spec = lax.optimization_barrier((recv, shot_spec))
    half = rows // 2
    first, second = moves(
        [recv],
        [(0, (every, every, pl.ds(k * half, half)), k, every) for k in range(2)],
        [(16, 2, half, depth)] * 2,
        pltpu.VMEM,
        pl.ANY,
    )
    first_left, second_right = shift(first, "x", 4, 1), shift(second, "x", 4, -1)
    first_left, second_right = ordered(first_left), ordered(second_right)
    far = {(2, 0): shift(first_left, "x", 4, 1), (2, half): shift(second_right, "x", 4, -1)}
    first_right = ordered(shift(first, "x", 4, -1))
    second_left = ordered(shift(second, "x", 4, 1))
    shots = by_frequency(shot_spec.swapaxes(0, 1))
    other = shift(shots, "c", 2, 1)
    near = {(0, 0): first, (0, half): second, (3, 0): first_left, (3, half): second_left}
    near |= {(1, 0): first_right, (1, half): second_right}
    out, own_p = product(place, wavelet, near, {0: shots}, rows, pack=True)
    out, other_p = product(place, wavelet, near, {1: other}, rows, out, pack=True)
    factors = {0: own_p, 1: other_p}
    (out,) = product(place, wavelet, far, factors, rows, out)
    out = back(out)
    (out,) = moves(
        [out],
        [
            (0, (every, core, every, part), 0, (part, every, every, core))
            for part in range(2)
            for core in range(2)
        ],
        [(2, 4, 4, 2) + out.shape[4:]],
        pltpu.VMEM,
        pl.ANY,
    )
    out = out.reshape((2, 16, -1, out.shape[-1]))
    return out.swapaxes(2, 3)


def back(out):
    out = out.reshape((-1,) + out.shape[4:])
    out = lax.all_to_all(out, PLACES, 0, 0, tiled=True)
    return out.reshape((4, 2, 4) + out.shape[1:])


def solution(mesh):
    devices = mesh.devices.reshape(2, 4, 2, 2, 4)
    wide = Mesh(devices, ("yh", "x", "c", "yl", "z"))
    spec = P(None, None, ("yh", "x", "c"), ("yl", "z"))
    return jax.shard_map(
        on_device, mesh=wide, in_specs=(spec, spec, P()), out_specs=spec, check_vma=False
    )
```

```python
import functools

import jax
import jax.numpy as jnp
from jax import lax
from jax.experimental import pallas as pl
from jax.experimental.pallas import tpu as pltpu
from jax.sharding import Mesh
from jax.sharding import PartitionSpec as P

FREQUENCY = ("z", "yl", "yh")
PLACES = ("z", "yl", "c", "yh")
ORDER = 2 * 10**10


def rows_of(piece, half):
    groups = piece.shape[0] // 2
    return jnp.concatenate(
        [piece[2 * j + half].reshape(-1, piece.shape[3]) for j in range(groups)], axis=1
    )


def emit(terms, spots, pieces, p_half, to_core, place, wave, out):
    shots = terms.shape[1] // 2
    x, frequency = place[0], place[2]
    w_real, w_imag = wave[0, frequency], wave[1, frequency]
    at = 0
    for (step, low), piece in zip(spots, pieces):
        rows = piece.shape[2]
        to = lax.rem(x + step, 4)
        for half in range(2):
            real, imag = terms[at : at + rows], terms[at + rows : at + 2 * rows]
            at += 2 * rows
            s_real = real[:, :shots] - imag[:, shots:]
            s_imag = real[:, shots:] + imag[:, :shots]
            out[to, half, to_core, p_half, 0, low : low + rows] = (
                w_real * s_real - w_imag * s_imag
            ).astype(out.dtype)
            out[to, half, to_core, p_half, 1, low : low + rows] = (
                w_real * s_imag + w_imag * s_real
            ).astype(out.dtype)


def product_kernel(spots, distances, pack, earlier, place, wave, *refs):
    pieces, refs = refs[: len(spots)], refs[len(spots) :]
    factors = refs[: len(distances)]
    out, *packed = refs[len(distances) + earlier :]
    for distance, factor in zip(distances, factors):
        to_core = lax.rem(place[1] + distance, 2)
        for p_half in range(2):
            if len(factor.shape) == 4:
                right_factor = rows_of(factor, p_half)
            else:
                right_factor = factor[p_half]
            if pack:
                packed[distance - distances[0]][p_half] = right_factor
            left_factor = jnp.concatenate(
                [rows_of(piece, half) for piece in pieces for half in range(2)], axis=0
            )
            terms = lax.dot_general(
                left_factor,
                right_factor,
                (((1,), (1,)), ((), ())),
                preferred_element_type=jnp.float32,
            )
            emit(terms, spots, pieces, p_half, to_core, place, wave, out)


def product(place, wavelet, blocks, factors, rows, earlier=None, pack=False):
    spots, pieces = tuple(blocks), list(blocks.values())
    distances, factors = tuple(factors), list(factors.values())
    depth = pieces[0].shape[0] // 2 * pieces[0].shape[3]
    shots = factors[0].shape[2] if factors[0].ndim == 4 else factors[0].shape[1] // 2
    vmem = pl.BlockSpec(memory_space=pltpu.VMEM)
    smem = pl.BlockSpec(memory_space=pltpu.SMEM)
    operands = [place, wavelet, *pieces, *factors]
    shapes = [jax.ShapeDtypeStruct((4, 2, 2, 2, 2, rows, shots), jnp.bfloat16)]
    if pack:
        shapes += [jax.ShapeDtypeStruct((2, 2 * shots, depth), jnp.bfloat16)] * len(factors)
    aliases = {}
    if earlier is not None:
        aliases = {len(operands): 0}
        operands.append(earlier)
    count = sum(piece.shape[2] for piece in pieces)
    flops = 2 * (4 * count) * (4 * shots * len(factors)) * depth
    return pl.pallas_call(
        functools.partial(product_kernel, spots, distances, pack, len(aliases)),
        out_shape=shapes,
        in_specs=[smem, smem] + [vmem] * (len(operands) - 2),
        out_specs=[vmem] * len(shapes),
        input_output_aliases=aliases,
        compiler_params=pltpu.CompilerParams(vmem_limit_bytes=28 * 2**20),
        cost_estimate=pl.CostEstimate(flops=flops, bytes_accessed=2**20, transcendentals=0),
    )(*operands)


def moves_kernel(pairs, count, *refs):
    sources, outs, done = refs[:count], refs[count:-1], refs[-1]
    copies = [
        pltpu.make_async_copy(sources[n].at[a], outs[k].at[b], done.at[i])
        for i, (n, a, k, b) in enumerate(pairs)
    ]
    for copy in copies:
        copy.start()
    for copy in copies:
        copy.wait()


def moves(values, pairs, shapes, source_space, out_space):
    outs = [jax.ShapeDtypeStruct(shape, values[0].dtype) for shape in shapes]
    return pl.pallas_call(
        functools.partial(moves_kernel, pairs, len(values)),
        out_shape=outs,
        in_specs=[pl.BlockSpec(memory_space=source_space)] * len(values),
        out_specs=[pl.BlockSpec(memory_space=out_space)] * len(outs),
        scratch_shapes=[pltpu.SemaphoreType.DMA((len(pairs),))],
        compiler_params=pltpu.CompilerParams(vmem_limit_bytes=8 * 2**20),
        cost_estimate=pl.CostEstimate(
            flops=0, bytes_accessed=4 * sum(value.size for value in values), transcendentals=0
        ),
    )(*values)


def ordered_kernel(source, out):
    pass


def ordered(value):
    return pl.pallas_call(
        ordered_kernel,
        out_shape=jax.ShapeDtypeStruct(value.shape, value.dtype),
        in_specs=[pl.BlockSpec(memory_space=pl.ANY)],
        out_specs=pl.BlockSpec(memory_space=pl.ANY),
        input_output_aliases={0: 0},
        cost_estimate=pl.CostEstimate(flops=ORDER, bytes_accessed=0, transcendentals=0),
    )(value)


def shift(value, axis, size, step):
    return lax.ppermute(value, axis, [(i, (i + step) % size) for i in range(size)])


def by_frequency(value):
    return lax.all_to_all(value, FREQUENCY, 0, 0, tiled=True)


def on_device(shot_spec, recv_spec, wavelet):
    place = jnp.stack(
        [lax.axis_index("x"), lax.axis_index("c"), lax.axis_index(FREQUENCY)]
    ).astype(jnp.int32)
    rows, depth = recv_spec.shape[2:]
    every = slice(None)
    (recv,) = moves(
        [recv_spec],
        [(0, part, 0, (every, part)) for part in range(2)],
        [(16, 2, rows, depth)],
        pltpu.HBM,
        pltpu.VMEM,
    )
    recv = by_frequency(recv)
    recv, shot_spec = lax.optimization_barrier((recv, shot_spec))
    half = rows // 2
    first, second = moves(
        [recv],
        [(0, (every, every, pl.ds(k * half, half)), k, every) for k in range(2)],
        [(16, 2, half, depth)] * 2,
        pltpu.VMEM,
        pl.ANY,
    )
    first_left, second_right = shift(first, "x", 4, 1), shift(second, "x", 4, -1)
    first_left, second_right = ordered(first_left), ordered(second_right)
    far = {(2, 0): shift(first_left, "x", 4, 1), (2, half): shift(second_right, "x", 4, -1)}
    first_right = ordered(shift(first, "x", 4, -1))
    second_left = ordered(shift(second, "x", 4, 1))
    shots = by_frequency(shot_spec.swapaxes(0, 1))
    other = shift(shots, "c", 2, 1)
    near = {(0, 0): first, (0, half): second, (3, 0): first_left, (3, half): second_left}
    near |= {(1, 0): first_right, (1, half): second_right}
    out, own_p = product(place, wavelet, near, {0: shots}, rows, pack=True)
    out, other_p = product(place, wavelet, near, {1: other}, rows, out, pack=True)
    factors = {0: own_p, 1: other_p}
    (out,) = product(place, wavelet, far, factors, rows, out)
    out = back(out)
    (out,) = moves(
        [out],
        [
            (0, (every, core, every, part), 0, (part, every, every, core))
            for part in range(2)
            for core in range(2)
        ],
        [(2, 8, 2, 2) + out.shape[4:]],
        pltpu.VMEM,
        pl.ANY,
    )
    out = out.reshape((2, 16, -1, out.shape[-1]))
    return out.swapaxes(2, 3)


def back(out):
    out = out.reshape((-1,) + out.shape[4:])
    out = lax.all_to_all(out, PLACES, 0, 0, tiled=True)
    return out.reshape((8, 2, 2) + out.shape[1:])


def solution(mesh):
    devices = mesh.devices.reshape(2, 4, 2, 2, 4)
    wide = Mesh(devices, ("yh", "x", "c", "yl", "z"))
    spec = P(None, None, ("yh", "x", "c"), ("yl", "z"))
    return jax.shard_map(
        on_device, mesh=wide, in_specs=(spec, spec, P()), out_specs=spec, check_vma=False
    )
```

```python
import functools

import jax
import jax.numpy as jnp
from jax import lax
from jax.experimental import pallas as pl
from jax.experimental.pallas import tpu as pltpu
from jax.sharding import Mesh
from jax.sharding import PartitionSpec as P

FREQUENCY = ("z", "yl", "yh")
PLACES = ("z", "yh", "c", "yl")
ORDER = 2 * 10**10


def rows_of(piece, half):
    groups = piece.shape[0] // 2
    return jnp.concatenate(
        [piece[2 * j + half].reshape(-1, piece.shape[3]) for j in range(groups)], axis=1
    )


def emit(terms, spots, pieces, p_half, to_core, place, wave, out):
    shots = terms.shape[1] // 2
    x, frequency = place[0], place[2]
    w_real, w_imag = wave[0, frequency], wave[1, frequency]
    at = 0
    for (step, low), piece in zip(spots, pieces):
        rows = piece.shape[2]
        to = lax.rem(x + step, 4)
        for half in range(2):
            real, imag = terms[at : at + rows], terms[at + rows : at + 2 * rows]
            at += 2 * rows
            s_real = real[:, :shots] - imag[:, shots:]
            s_imag = real[:, shots:] + imag[:, :shots]
            out[to, p_half, to_core, half, 0, low : low + rows] = (
                w_real * s_real - w_imag * s_imag
            ).astype(out.dtype)
            out[to, p_half, to_core, half, 1, low : low + rows] = (
                w_real * s_imag + w_imag * s_real
            ).astype(out.dtype)


def product_kernel(spots, distances, pack, earlier, place, wave, *refs):
    pieces, refs = refs[: len(spots)], refs[len(spots) :]
    factors = refs[: len(distances)]
    out, *packed = refs[len(distances) + earlier :]
    for distance, factor in zip(distances, factors):
        to_core = lax.rem(place[1] + distance, 2)
        for p_half in range(2):
            if len(factor.shape) == 4:
                right_factor = rows_of(factor, p_half)
            else:
                right_factor = factor[p_half]
            if pack:
                packed[distance - distances[0]][p_half] = right_factor
            left_factor = jnp.concatenate(
                [rows_of(piece, half) for piece in pieces for half in range(2)], axis=0
            )
            terms = lax.dot_general(
                left_factor,
                right_factor,
                (((1,), (1,)), ((), ())),
                preferred_element_type=jnp.float32,
            )
            emit(terms, spots, pieces, p_half, to_core, place, wave, out)


def product(place, wavelet, blocks, factors, rows, earlier=None, pack=False):
    spots, pieces = tuple(blocks), list(blocks.values())
    distances, factors = tuple(factors), list(factors.values())
    depth = pieces[0].shape[0] // 2 * pieces[0].shape[3]
    shots = factors[0].shape[2] if factors[0].ndim == 4 else factors[0].shape[1] // 2
    vmem = pl.BlockSpec(memory_space=pltpu.VMEM)
    smem = pl.BlockSpec(memory_space=pltpu.SMEM)
    operands = [place, wavelet, *pieces, *factors]
    shapes = [jax.ShapeDtypeStruct((4, 2, 2, 2, 2, rows, shots), jnp.bfloat16)]
    if pack:
        shapes += [jax.ShapeDtypeStruct((2, 2 * shots, depth), jnp.bfloat16)] * len(factors)
    aliases = {}
    if earlier is not None:
        aliases = {len(operands): 0}
        operands.append(earlier)
    count = sum(piece.shape[2] for piece in pieces)
    flops = 2 * (4 * count) * (4 * shots * len(factors)) * depth
    return pl.pallas_call(
        functools.partial(product_kernel, spots, distances, pack, len(aliases)),
        out_shape=shapes,
        in_specs=[smem, smem] + [vmem] * (len(operands) - 2),
        out_specs=[vmem] * len(shapes),
        input_output_aliases=aliases,
        compiler_params=pltpu.CompilerParams(vmem_limit_bytes=28 * 2**20),
        cost_estimate=pl.CostEstimate(flops=flops, bytes_accessed=2**20, transcendentals=0),
    )(*operands)


def moves_kernel(pairs, count, *refs):
    sources, outs, done = refs[:count], refs[count:-1], refs[-1]
    copies = [
        pltpu.make_async_copy(sources[n].at[a], outs[k].at[b], done.at[i])
        for i, (n, a, k, b) in enumerate(pairs)
    ]
    for copy in copies:
        copy.start()
    for copy in copies:
        copy.wait()


def moves(values, pairs, shapes, source_space, out_space):
    outs = [jax.ShapeDtypeStruct(shape, values[0].dtype) for shape in shapes]
    return pl.pallas_call(
        functools.partial(moves_kernel, pairs, len(values)),
        out_shape=outs,
        in_specs=[pl.BlockSpec(memory_space=source_space)] * len(values),
        out_specs=[pl.BlockSpec(memory_space=out_space)] * len(outs),
        scratch_shapes=[pltpu.SemaphoreType.DMA((len(pairs),))],
        compiler_params=pltpu.CompilerParams(vmem_limit_bytes=8 * 2**20),
        cost_estimate=pl.CostEstimate(
            flops=0, bytes_accessed=4 * sum(value.size for value in values), transcendentals=0
        ),
    )(*values)


def ordered_kernel(source, out):
    pass


def ordered(value):
    return pl.pallas_call(
        ordered_kernel,
        out_shape=jax.ShapeDtypeStruct(value.shape, value.dtype),
        in_specs=[pl.BlockSpec(memory_space=pl.ANY)],
        out_specs=pl.BlockSpec(memory_space=pl.ANY),
        input_output_aliases={0: 0},
        cost_estimate=pl.CostEstimate(flops=ORDER, bytes_accessed=0, transcendentals=0),
    )(value)


def shift(value, axis, size, step):
    return lax.ppermute(value, axis, [(i, (i + step) % size) for i in range(size)])


def by_frequency(value):
    return lax.all_to_all(value, FREQUENCY, 0, 0, tiled=True)


def on_device(shot_spec, recv_spec, wavelet):
    place = jnp.stack(
        [lax.axis_index("x"), lax.axis_index("c"), lax.axis_index(FREQUENCY)]
    ).astype(jnp.int32)
    rows, depth = recv_spec.shape[2:]
    every = slice(None)
    (recv,) = moves(
        [recv_spec],
        [(0, part, 0, (every, part)) for part in range(2)],
        [(16, 2, rows, depth)],
        pltpu.HBM,
        pltpu.VMEM,
    )
    recv = by_frequency(recv)
    recv, shot_spec = lax.optimization_barrier((recv, shot_spec))
    half = rows // 2
    first, second = moves(
        [recv],
        [(0, (every, every, pl.ds(k * half, half)), k, every) for k in range(2)],
        [(16, 2, half, depth)] * 2,
        pltpu.VMEM,
        pl.ANY,
    )
    first_left, second_right = shift(first, "x", 4, 1), shift(second, "x", 4, -1)
    first_left, second_right = ordered(first_left), ordered(second_right)
    far = {(2, 0): shift(first_left, "x", 4, 1), (2, half): shift(second_right, "x", 4, -1)}
    first_right = ordered(shift(first, "x", 4, -1))
    second_left = ordered(shift(second, "x", 4, 1))
    shots = by_frequency(shot_spec.swapaxes(0, 1))
    other = shift(shots, "c", 2, 1)
    near = {(0, 0): first, (0, half): second, (3, 0): first_left, (3, half): second_left}
    near |= {(1, 0): first_right, (1, half): second_right}
    out, own_p = product(place, wavelet, near, {0: shots}, rows, pack=True)
    out, other_p = product(place, wavelet, near, {1: other}, rows, out, pack=True)
    factors = {0: own_p, 1: other_p}
    (out,) = product(place, wavelet, far, factors, rows, out)
    out = back(out)
    (out,) = moves(
        [out],
        [
            (0, (every, yh, core, every, part), 0, (part, every, every, yh, core))
            for part in range(2)
            for core in range(2)
            for yh in range(2)
        ],
        [(2, 4, 2, 2, 2) + out.shape[5:]],
        pltpu.VMEM,
        pl.ANY,
    )
    out = out.reshape((2, 16, -1, out.shape[-1]))
    return out.swapaxes(2, 3)


def back(out):
    out = out.reshape((-1,) + out.shape[4:])
    out = lax.all_to_all(out, PLACES, 0, 0, tiled=True)
    return out.reshape((4, 2, 2, 2) + out.shape[1:])


def solution(mesh):
    devices = mesh.devices.reshape(2, 4, 2, 2, 4)
    wide = Mesh(devices, ("yh", "x", "c", "yl", "z"))
    spec = P(None, None, ("yh", "x", "c"), ("yl", "z"))
    return jax.shard_map(
        on_device, mesh=wide, in_specs=(spec, spec, P()), out_specs=spec, check_vma=False
    )
```

```python
import functools

import jax
import jax.numpy as jnp
from jax import lax
from jax.experimental import pallas as pl
from jax.experimental.pallas import tpu as pltpu
from jax.sharding import Mesh
from jax.sharding import PartitionSpec as P

FREQUENCY = ("z", "yl", "yh")
PLACES = ("z", "yl", "c", "yh")
ORDER = 2 * 10**10


def rows_of(piece, half):
    groups = piece.shape[0] // 2
    return jnp.concatenate(
        [piece[2 * j + half].reshape(-1, piece.shape[3]) for j in range(groups)], axis=1
    )


def emit(terms, spots, pieces, p_half, to_core, place, wave, out):
    shots = terms.shape[1] // 2
    x, frequency = place[0], place[2]
    w_real, w_imag = wave[0, frequency], wave[1, frequency]
    at = 0
    for (step, low), piece in zip(spots, pieces):
        rows = piece.shape[2]
        to = lax.rem(x + step, 4)
        for half in range(2):
            real, imag = terms[at : at + rows], terms[at + rows : at + 2 * rows]
            at += 2 * rows
            s_real = real[:, :shots] - imag[:, shots:]
            s_imag = real[:, shots:] + imag[:, :shots]
            out[to, half, to_core, p_half, 0, low : low + rows] = (
                w_real * s_real - w_imag * s_imag
            ).astype(out.dtype)
            out[to, half, to_core, p_half, 1, low : low + rows] = (
                w_real * s_imag + w_imag * s_real
            ).astype(out.dtype)


def product_kernel(spots, distances, pack, earlier, place, wave, *refs):
    pieces, refs = refs[: len(spots)], refs[len(spots) :]
    factors = refs[: len(distances)]
    out, *packed = refs[len(distances) + earlier :]
    if not pack:
        left_factor = jnp.concatenate(
            [rows_of(piece, half) for piece in pieces for half in range(2)], axis=0
        )
        rights = []
        for distance, factor in zip(distances, factors):
            for p_half in range(2):
                right_factor = rows_of(factor, p_half) if len(factor.shape) == 4 else factor[p_half]
                if pack:
                    packed[distance - distances[0]][p_half] = right_factor
                rights.append(right_factor)
        terms = lax.dot_general(
            left_factor,
            jnp.concatenate(rights, axis=0),
            (((1,), (1,)), ((), ())),
            preferred_element_type=jnp.float32,
        )
        width = rights[0].shape[0]
        for i, distance in enumerate(distances):
            to_core = lax.rem(place[1] + distance, 2)
            for p_half in range(2):
                at = (2 * i + p_half) * width
                emit(terms[:, at : at + width], spots, pieces, p_half, to_core, place, wave, out)
        return
    for distance, factor in zip(distances, factors):
        to_core = lax.rem(place[1] + distance, 2)
        for p_half in range(2):
            if len(factor.shape) == 4:
                right_factor = rows_of(factor, p_half)
            else:
                right_factor = factor[p_half]
            if pack:
                packed[distance - distances[0]][p_half] = right_factor
            left_factor = jnp.concatenate(
                [rows_of(piece, half) for piece in pieces for half in range(2)], axis=0
            )
            terms = lax.dot_general(
                left_factor,
                right_factor,
                (((1,), (1,)), ((), ())),
                preferred_element_type=jnp.float32,
            )
            emit(terms, spots, pieces, p_half, to_core, place, wave, out)


def product(place, wavelet, blocks, factors, rows, earlier=None, pack=False):
    spots, pieces = tuple(blocks), list(blocks.values())
    distances, factors = tuple(factors), list(factors.values())
    depth = pieces[0].shape[0] // 2 * pieces[0].shape[3]
    shots = factors[0].shape[2] if factors[0].ndim == 4 else factors[0].shape[1] // 2
    vmem = pl.BlockSpec(memory_space=pltpu.VMEM)
    smem = pl.BlockSpec(memory_space=pltpu.SMEM)
    operands = [place, wavelet, *pieces, *factors]
    shapes = [jax.ShapeDtypeStruct((4, 2, 2, 2, 2, rows, shots), jnp.bfloat16)]
    if pack:
        shapes += [jax.ShapeDtypeStruct((2, 2 * shots, depth), jnp.bfloat16)] * len(factors)
    aliases = {}
    if earlier is not None:
        aliases = {len(operands): 0}
        operands.append(earlier)
    count = sum(piece.shape[2] for piece in pieces)
    flops = 2 * (4 * count) * (4 * shots * len(factors)) * depth
    return pl.pallas_call(
        functools.partial(product_kernel, spots, distances, pack, len(aliases)),
        out_shape=shapes,
        in_specs=[smem, smem] + [vmem] * (len(operands) - 2),
        out_specs=[vmem] * len(shapes),
        input_output_aliases=aliases,
        compiler_params=pltpu.CompilerParams(vmem_limit_bytes=28 * 2**20),
        cost_estimate=pl.CostEstimate(flops=flops, bytes_accessed=2**20, transcendentals=0),
    )(*operands)


def moves_kernel(pairs, count, *refs):
    sources, outs, done = refs[:count], refs[count:-1], refs[-1]
    copies = [
        pltpu.make_async_copy(sources[n].at[a], outs[k].at[b], done.at[i])
        for i, (n, a, k, b) in enumerate(pairs)
    ]
    for copy in copies:
        copy.start()
    for copy in copies:
        copy.wait()


def moves(values, pairs, shapes, source_space, out_space):
    outs = [jax.ShapeDtypeStruct(shape, values[0].dtype) for shape in shapes]
    return pl.pallas_call(
        functools.partial(moves_kernel, pairs, len(values)),
        out_shape=outs,
        in_specs=[pl.BlockSpec(memory_space=source_space)] * len(values),
        out_specs=[pl.BlockSpec(memory_space=out_space)] * len(outs),
        scratch_shapes=[pltpu.SemaphoreType.DMA((len(pairs),))],
        compiler_params=pltpu.CompilerParams(vmem_limit_bytes=8 * 2**20),
        cost_estimate=pl.CostEstimate(
            flops=0, bytes_accessed=4 * sum(value.size for value in values), transcendentals=0
        ),
    )(*values)


def ordered_kernel(source, out):
    pass


def ordered(value):
    return pl.pallas_call(
        ordered_kernel,
        out_shape=jax.ShapeDtypeStruct(value.shape, value.dtype),
        in_specs=[pl.BlockSpec(memory_space=pl.ANY)],
        out_specs=pl.BlockSpec(memory_space=pl.ANY),
        input_output_aliases={0: 0},
        cost_estimate=pl.CostEstimate(flops=ORDER, bytes_accessed=0, transcendentals=0),
    )(value)


def shift(value, axis, size, step):
    return lax.ppermute(value, axis, [(i, (i + step) % size) for i in range(size)])


def by_frequency(value):
    return lax.all_to_all(value, FREQUENCY, 0, 0, tiled=True)


def on_device(shot_spec, recv_spec, wavelet):
    place = jnp.stack(
        [lax.axis_index("x"), lax.axis_index("c"), lax.axis_index(FREQUENCY)]
    ).astype(jnp.int32)
    rows, depth = recv_spec.shape[2:]
    every = slice(None)
    (recv,) = moves(
        [recv_spec],
        [(0, part, 0, (every, part)) for part in range(2)],
        [(16, 2, rows, depth)],
        pltpu.HBM,
        pltpu.VMEM,
    )
    recv = by_frequency(recv)
    recv, shot_spec = lax.optimization_barrier((recv, shot_spec))
    half = rows // 2
    first, second = moves(
        [recv],
        [(0, (every, every, pl.ds(k * half, half)), k, every) for k in range(2)],
        [(16, 2, half, depth)] * 2,
        pltpu.VMEM,
        pl.ANY,
    )
    first_left, second_right = shift(first, "x", 4, 1), shift(second, "x", 4, -1)
    first_left, second_right = ordered(first_left), ordered(second_right)
    far = {(2, 0): shift(first_left, "x", 4, 1), (2, half): shift(second_right, "x", 4, -1)}
    first_right = ordered(shift(first, "x", 4, -1))
    second_left = ordered(shift(second, "x", 4, 1))
    shots = by_frequency(shot_spec.swapaxes(0, 1))
    other = shift(shots, "c", 2, 1)
    near = {(0, 0): first, (0, half): second, (3, 0): first_left, (3, half): second_left}
    near |= {(1, 0): first_right, (1, half): second_right}
    out, own_p = product(place, wavelet, near, {0: shots}, rows, pack=True)
    out, other_p = product(place, wavelet, near, {1: other}, rows, out, pack=True)
    factors = {0: own_p, 1: other_p}
    (out,) = product(place, wavelet, far, factors, rows, out)
    out = back(out)
    (out,) = moves(
        [out],
        [
            (0, (every, core, every, part), 0, (part, every, every, core))
            for part in range(2)
            for core in range(2)
        ],
        [(2, 8, 2, 2) + out.shape[4:]],
        pltpu.VMEM,
        pl.ANY,
    )
    out = out.reshape((2, 16, -1, out.shape[-1]))
    return out.swapaxes(2, 3)


def back(out):
    out = out.reshape((-1,) + out.shape[4:])
    out = lax.all_to_all(out, PLACES, 0, 0, tiled=True)
    return out.reshape((8, 2, 2) + out.shape[1:])


def solution(mesh):
    devices = mesh.devices.reshape(2, 4, 2, 2, 4)
    wide = Mesh(devices, ("yh", "x", "c", "yl", "z"))
    spec = P(None, None, ("yh", "x", "c"), ("yl", "z"))
    return jax.shard_map(
        on_device, mesh=wide, in_specs=(spec, spec, P()), out_specs=spec, check_vma=False
    )
```

```python
import functools

import jax
import jax.numpy as jnp
from jax import lax
from jax.experimental import pallas as pl
from jax.experimental.pallas import tpu as pltpu
from jax.sharding import Mesh
from jax.sharding import PartitionSpec as P

FREQUENCY = ("z", "yl", "yh")
PLACES = ("z", "yh", "c", "yl")
ORDER = 2 * 10**10


def rows_of(piece, half):
    groups = piece.shape[0] // 2
    return jnp.concatenate(
        [piece[2 * j + half].reshape(-1, piece.shape[3]) for j in range(groups)], axis=1
    )


def emit(terms, spots, pieces, p_half, to_core, place, wave, out):
    shots = terms.shape[1] // 2
    x, frequency = place[0], place[2]
    w_real, w_imag = wave[0, frequency], wave[1, frequency]
    at = 0
    for (step, low), piece in zip(spots, pieces):
        rows = piece.shape[2]
        to = lax.rem(x + step, 4)
        for half in range(2):
            real, imag = terms[at : at + rows], terms[at + rows : at + 2 * rows]
            at += 2 * rows
            s_real = real[:, :shots] - imag[:, shots:]
            s_imag = real[:, shots:] + imag[:, :shots]
            out[to, p_half, to_core, half, 0, low : low + rows] = (
                w_real * s_real - w_imag * s_imag
            ).astype(out.dtype)
            out[to, p_half, to_core, half, 1, low : low + rows] = (
                w_real * s_imag + w_imag * s_real
            ).astype(out.dtype)


def product_kernel(spots, distances, pack, earlier, place, wave, *refs):
    pieces, refs = refs[: len(spots)], refs[len(spots) :]
    factors = refs[: len(distances)]
    out, *packed = refs[len(distances) + earlier :]
    if not pack:
        left_factor = jnp.concatenate(
            [rows_of(piece, half) for piece in pieces for half in range(2)], axis=0
        )
        rights = []
        for distance, factor in zip(distances, factors):
            for p_half in range(2):
                right_factor = rows_of(factor, p_half) if len(factor.shape) == 4 else factor[p_half]
                if pack:
                    packed[distance - distances[0]][p_half] = right_factor
                rights.append(right_factor)
        terms = lax.dot_general(
            left_factor,
            jnp.concatenate(rights, axis=0),
            (((1,), (1,)), ((), ())),
            preferred_element_type=jnp.float32,
        )
        width = rights[0].shape[0]
        for i, distance in enumerate(distances):
            to_core = lax.rem(place[1] + distance, 2)
            for p_half in range(2):
                at = (2 * i + p_half) * width
                emit(terms[:, at : at + width], spots, pieces, p_half, to_core, place, wave, out)
        return
    for distance, factor in zip(distances, factors):
        to_core = lax.rem(place[1] + distance, 2)
        for p_half in range(2):
            if len(factor.shape) == 4:
                right_factor = rows_of(factor, p_half)
            else:
                right_factor = factor[p_half]
            if pack:
                packed[distance - distances[0]][p_half] = right_factor
            left_factor = jnp.concatenate(
                [rows_of(piece, half) for piece in pieces for half in range(2)], axis=0
            )
            terms = lax.dot_general(
                left_factor,
                right_factor,
                (((1,), (1,)), ((), ())),
                preferred_element_type=jnp.float32,
            )
            emit(terms, spots, pieces, p_half, to_core, place, wave, out)


def product(place, wavelet, blocks, factors, rows, earlier=None, pack=False):
    spots, pieces = tuple(blocks), list(blocks.values())
    distances, factors = tuple(factors), list(factors.values())
    depth = pieces[0].shape[0] // 2 * pieces[0].shape[3]
    shots = factors[0].shape[2] if factors[0].ndim == 4 else factors[0].shape[1] // 2
    vmem = pl.BlockSpec(memory_space=pltpu.VMEM)
    smem = pl.BlockSpec(memory_space=pltpu.SMEM)
    operands = [place, wavelet, *pieces, *factors]
    shapes = [jax.ShapeDtypeStruct((4, 2, 2, 2, 2, rows, shots), jnp.bfloat16)]
    if pack:
        shapes += [jax.ShapeDtypeStruct((2, 2 * shots, depth), jnp.bfloat16)] * len(factors)
    aliases = {}
    if earlier is not None:
        aliases = {len(operands): 0}
        operands.append(earlier)
    count = sum(piece.shape[2] for piece in pieces)
    flops = 2 * (4 * count) * (4 * shots * len(factors)) * depth
    return pl.pallas_call(
        functools.partial(product_kernel, spots, distances, pack, len(aliases)),
        out_shape=shapes,
        in_specs=[smem, smem] + [vmem] * (len(operands) - 2),
        out_specs=[vmem] * len(shapes),
        input_output_aliases=aliases,
        compiler_params=pltpu.CompilerParams(vmem_limit_bytes=28 * 2**20),
        cost_estimate=pl.CostEstimate(flops=flops, bytes_accessed=2**20, transcendentals=0),
    )(*operands)


def moves_kernel(pairs, count, *refs):
    sources, outs, done = refs[:count], refs[count:-1], refs[-1]
    copies = [
        pltpu.make_async_copy(sources[n].at[a], outs[k].at[b], done.at[i])
        for i, (n, a, k, b) in enumerate(pairs)
    ]
    for copy in copies:
        copy.start()
    for copy in copies:
        copy.wait()


def moves(values, pairs, shapes, source_space, out_space):
    outs = [jax.ShapeDtypeStruct(shape, values[0].dtype) for shape in shapes]
    return pl.pallas_call(
        functools.partial(moves_kernel, pairs, len(values)),
        out_shape=outs,
        in_specs=[pl.BlockSpec(memory_space=source_space)] * len(values),
        out_specs=[pl.BlockSpec(memory_space=out_space)] * len(outs),
        scratch_shapes=[pltpu.SemaphoreType.DMA((len(pairs),))],
        compiler_params=pltpu.CompilerParams(vmem_limit_bytes=8 * 2**20),
        cost_estimate=pl.CostEstimate(
            flops=0, bytes_accessed=4 * sum(value.size for value in values), transcendentals=0
        ),
    )(*values)


def ordered_kernel(source, out):
    pass


def ordered(value):
    return pl.pallas_call(
        ordered_kernel,
        out_shape=jax.ShapeDtypeStruct(value.shape, value.dtype),
        in_specs=[pl.BlockSpec(memory_space=pl.ANY)],
        out_specs=pl.BlockSpec(memory_space=pl.ANY),
        input_output_aliases={0: 0},
        cost_estimate=pl.CostEstimate(flops=ORDER, bytes_accessed=0, transcendentals=0),
    )(value)


def shift(value, axis, size, step):
    return lax.ppermute(value, axis, [(i, (i + step) % size) for i in range(size)])


def by_frequency(value):
    return lax.all_to_all(value, FREQUENCY, 0, 0, tiled=True)


def on_device(shot_spec, recv_spec, wavelet):
    place = jnp.stack(
        [lax.axis_index("x"), lax.axis_index("c"), lax.axis_index(FREQUENCY)]
    ).astype(jnp.int32)
    rows, depth = recv_spec.shape[2:]
    every = slice(None)
    (recv,) = moves(
        [recv_spec],
        [(0, part, 0, (every, part)) for part in range(2)],
        [(16, 2, rows, depth)],
        pltpu.HBM,
        pltpu.VMEM,
    )
    recv = by_frequency(recv)
    recv, shot_spec = lax.optimization_barrier((recv, shot_spec))
    half = rows // 2
    first, second = moves(
        [recv],
        [(0, (every, every, pl.ds(k * half, half)), k, every) for k in range(2)],
        [(16, 2, half, depth)] * 2,
        pltpu.VMEM,
        pl.ANY,
    )
    first_left, second_right = shift(first, "x", 4, 1), shift(second, "x", 4, -1)
    first_left, second_right = ordered(first_left), ordered(second_right)
    far = {(2, 0): shift(first_left, "x", 4, 1), (2, half): shift(second_right, "x", 4, -1)}
    first_right = ordered(shift(first, "x", 4, -1))
    second_left = ordered(shift(second, "x", 4, 1))
    shots = by_frequency(shot_spec.swapaxes(0, 1))
    other = shift(shots, "c", 2, 1)
    near = {(0, 0): first, (0, half): second, (3, 0): first_left, (3, half): second_left}
    near |= {(1, 0): first_right, (1, half): second_right}
    out, own_p = product(place, wavelet, near, {0: shots}, rows, pack=True)
    out, other_p = product(place, wavelet, near, {1: other}, rows, out, pack=True)
    factors = {0: own_p, 1: other_p}
    (out,) = product(place, wavelet, far, factors, rows, out)
    out = back(out)
    (out,) = moves(
        [out],
        [
            (0, (every, yh, core, every, part), 0, (part, every, every, yh, core))
            for part in range(2)
            for core in range(2)
            for yh in range(2)
        ],
        [(2, 4, 2, 2, 2) + out.shape[5:]],
        pltpu.VMEM,
        pl.ANY,
    )
    out = out.reshape((2, 16, -1, out.shape[-1]))
    return out.swapaxes(2, 3)


def back(out):
    out = out.reshape((-1,) + out.shape[4:])
    out = lax.all_to_all(out, PLACES, 0, 0, tiled=True)
    return out.reshape((4, 2, 2, 2) + out.shape[1:])


def solution(mesh):
    devices = mesh.devices.reshape(2, 4, 2, 2, 4)
    wide = Mesh(devices, ("yh", "x", "c", "yl", "z"))
    spec = P(None, None, ("yh", "x", "c"), ("yl", "z"))
    return jax.shard_map(
        on_device, mesh=wide, in_specs=(spec, spec, P()), out_specs=spec, check_vma=False
    )
```

```python
import functools

import jax
import jax.numpy as jnp
from jax import lax
from jax.experimental import pallas as pl
from jax.experimental.pallas import tpu as pltpu
from jax.sharding import Mesh
from jax.sharding import PartitionSpec as P

FREQUENCY = ("z", "yl", "yh")
PLACES = ("z", "yh", "c", "yl")
ORDER = 2 * 10**10


def rows_of(piece, half):
    groups = piece.shape[0] // 2
    return jnp.concatenate(
        [piece[2 * j + half].reshape(-1, piece.shape[3]) for j in range(groups)], axis=1
    )


def emit(terms, spots, pieces, p_half, to_core, place, wave, out):
    shots = terms.shape[1] // 2
    x, frequency = place[0], place[2]
    w_real, w_imag = wave[0, frequency], wave[1, frequency]
    at = 0
    for (step, low), piece in zip(spots, pieces):
        rows = piece.shape[2]
        to = lax.rem(x + step, 4)
        for half in range(2):
            real, imag = terms[at : at + rows], terms[at + rows : at + 2 * rows]
            at += 2 * rows
            s_real = real[:, :shots] - imag[:, shots:]
            s_imag = real[:, shots:] + imag[:, :shots]
            out[to, p_half, to_core, half, 0, low : low + rows] = (
                w_real * s_real - w_imag * s_imag
            ).astype(out.dtype)
            out[to, p_half, to_core, half, 1, low : low + rows] = (
                w_real * s_imag + w_imag * s_real
            ).astype(out.dtype)


def product_kernel(spots, distances, pack, earlier, place, wave, *refs):
    pieces, refs = refs[: len(spots)], refs[len(spots) :]
    factors = refs[: len(distances)]
    out, *packed = refs[len(distances) + earlier :]
    if not pack:
        left_factor = jnp.concatenate(
            [rows_of(piece, half) for piece in pieces for half in range(2)], axis=0
        )
        rights = []
        for distance, factor in zip(distances, factors):
            for p_half in range(2):
                right_factor = rows_of(factor, p_half) if len(factor.shape) == 4 else factor[p_half]
                if pack:
                    packed[distance - distances[0]][p_half] = right_factor
                rights.append(right_factor)
        terms = lax.dot_general(
            left_factor,
            jnp.concatenate(rights, axis=0),
            (((1,), (1,)), ((), ())),
            preferred_element_type=jnp.float32,
        )
        width = rights[0].shape[0]
        for i, distance in enumerate(distances):
            to_core = lax.rem(place[1] + distance, 2)
            for p_half in range(2):
                at = (2 * i + p_half) * width
                emit(terms[:, at : at + width], spots, pieces, p_half, to_core, place, wave, out)
        return
    for distance, factor in zip(distances, factors):
        to_core = lax.rem(place[1] + distance, 2)
        for p_half in range(2):
            if len(factor.shape) == 4:
                right_factor = rows_of(factor, p_half)
            else:
                right_factor = factor[p_half]
            if pack:
                packed[distance - distances[0]][p_half] = right_factor
            left_factor = jnp.concatenate(
                [rows_of(piece, half) for piece in pieces for half in range(2)], axis=0
            )
            terms = lax.dot_general(
                left_factor,
                right_factor,
                (((1,), (1,)), ((), ())),
                preferred_element_type=jnp.float32,
            )
            emit(terms, spots, pieces, p_half, to_core, place, wave, out)


def product(place, wavelet, blocks, factors, rows, earlier=None, pack=False):
    spots, pieces = tuple(blocks), list(blocks.values())
    distances, factors = tuple(factors), list(factors.values())
    depth = pieces[0].shape[0] // 2 * pieces[0].shape[3]
    shots = factors[0].shape[2] if factors[0].ndim == 4 else factors[0].shape[1] // 2
    vmem = pl.BlockSpec(memory_space=pltpu.VMEM)
    smem = pl.BlockSpec(memory_space=pltpu.SMEM)
    operands = [place, wavelet, *pieces, *factors]
    shapes = [jax.ShapeDtypeStruct((4, 2, 2, 2, 2, rows, shots), jnp.bfloat16)]
    if pack:
        shapes += [jax.ShapeDtypeStruct((2, 2 * shots, depth), jnp.bfloat16)] * len(factors)
    aliases = {}
    if earlier is not None:
        aliases = {len(operands): 0}
        operands.append(earlier)
    count = sum(piece.shape[2] for piece in pieces)
    flops = 2 * (4 * count) * (4 * shots * len(factors)) * depth
    return pl.pallas_call(
        functools.partial(product_kernel, spots, distances, pack, len(aliases)),
        out_shape=shapes,
        in_specs=[smem, smem] + [vmem] * (len(operands) - 2),
        out_specs=[vmem] * len(shapes),
        input_output_aliases=aliases,
        compiler_params=pltpu.CompilerParams(vmem_limit_bytes=14 * 2**20),
        cost_estimate=pl.CostEstimate(flops=flops, bytes_accessed=2**20, transcendentals=0),
    )(*operands)


def moves_kernel(pairs, count, *refs):
    sources, outs, done = refs[:count], refs[count:-1], refs[-1]
    copies = [
        pltpu.make_async_copy(sources[n].at[a], outs[k].at[b], done.at[i])
        for i, (n, a, k, b) in enumerate(pairs)
    ]
    for copy in copies:
        copy.start()
    for copy in copies:
        copy.wait()


def moves(values, pairs, shapes, source_space, out_space):
    outs = [jax.ShapeDtypeStruct(shape, values[0].dtype) for shape in shapes]
    return pl.pallas_call(
        functools.partial(moves_kernel, pairs, len(values)),
        out_shape=outs,
        in_specs=[pl.BlockSpec(memory_space=source_space)] * len(values),
        out_specs=[pl.BlockSpec(memory_space=out_space)] * len(outs),
        scratch_shapes=[pltpu.SemaphoreType.DMA((len(pairs),))],
        compiler_params=pltpu.CompilerParams(vmem_limit_bytes=8 * 2**20),
        cost_estimate=pl.CostEstimate(
            flops=0, bytes_accessed=4 * sum(value.size for value in values), transcendentals=0
        ),
    )(*values)


def ordered_kernel(source, out):
    pass


def ordered(value):
    return pl.pallas_call(
        ordered_kernel,
        out_shape=jax.ShapeDtypeStruct(value.shape, value.dtype),
        in_specs=[pl.BlockSpec(memory_space=pl.ANY)],
        out_specs=pl.BlockSpec(memory_space=pl.ANY),
        input_output_aliases={0: 0},
        cost_estimate=pl.CostEstimate(flops=ORDER, bytes_accessed=0, transcendentals=0),
    )(value)


def shift(value, axis, size, step):
    return lax.ppermute(value, axis, [(i, (i + step) % size) for i in range(size)])


def by_frequency(value):
    return lax.all_to_all(value, FREQUENCY, 0, 0, tiled=True)


def on_device(shot_spec, recv_spec, wavelet):
    place = jnp.stack(
        [lax.axis_index("x"), lax.axis_index("c"), lax.axis_index(FREQUENCY)]
    ).astype(jnp.int32)
    rows, depth = recv_spec.shape[2:]
    every = slice(None)
    (recv,) = moves(
        [recv_spec],
        [(0, part, 0, (every, part)) for part in range(2)],
        [(16, 2, rows, depth)],
        pltpu.HBM,
        pltpu.VMEM,
    )
    recv = by_frequency(recv)
    recv, shot_spec = lax.optimization_barrier((recv, shot_spec))
    half = rows // 2
    first, second = moves(
        [recv],
        [(0, (every, every, pl.ds(k * half, half)), k, every) for k in range(2)],
        [(16, 2, half, depth)] * 2,
        pltpu.VMEM,
        pl.ANY,
    )
    first_left, second_right = shift(first, "x", 4, 1), shift(second, "x", 4, -1)
    first_left, second_right = ordered(first_left), ordered(second_right)
    far = {(2, 0): shift(first_left, "x", 4, 1), (2, half): shift(second_right, "x", 4, -1)}
    first_right = ordered(shift(first, "x", 4, -1))
    second_left = ordered(shift(second, "x", 4, 1))
    shots = by_frequency(shot_spec.swapaxes(0, 1))
    other = shift(shots, "c", 2, 1)
    near = {(0, 0): first, (0, half): second, (3, 0): first_left, (3, half): second_left}
    near |= {(1, 0): first_right, (1, half): second_right}
    out, own_p = product(place, wavelet, near, {0: shots}, rows, pack=True)
    out, other_p = product(place, wavelet, near, {1: other}, rows, out, pack=True)
    factors = {0: own_p, 1: other_p}
    (out,) = product(place, wavelet, far, factors, rows, out)
    out = back(out)
    (out,) = moves(
        [out],
        [
            (0, (every, yh, core, every, part), 0, (part, every, every, yh, core))
            for part in range(2)
            for core in range(2)
            for yh in range(2)
        ],
        [(2, 4, 2, 2, 2) + out.shape[5:]],
        pltpu.VMEM,
        pl.ANY,
    )
    out = out.reshape((2, 16, -1, out.shape[-1]))
    return out.swapaxes(2, 3)


def back(out):
    out = out.reshape((-1,) + out.shape[4:])
    out = lax.all_to_all(out, PLACES, 0, 0, tiled=True)
    return out.reshape((4, 2, 2, 2) + out.shape[1:])


def solution(mesh):
    devices = mesh.devices.reshape(2, 4, 2, 2, 4)
    wide = Mesh(devices, ("yh", "x", "c", "yl", "z"))
    spec = P(None, None, ("yh", "x", "c"), ("yl", "z"))
    return jax.shard_map(
        on_device, mesh=wide, in_specs=(spec, spec, P()), out_specs=spec, check_vma=False
    )
```
